256 devices in a mesh: slab: 16 (over y, z_hi), filt: 16 (over x, z_lo, core).
Axes of the slice: x: 4, y: 4, z: 8 (z_hi: 4, z_lo: 2; z = z_hi * 2 + z_lo), core: 2. Of those that a mesh axis runs over, the one named last changes fastest.
Arguments:
- cotangent: bfloat16 [32, 16, 64, 256], P('slab', None, None, 'filt'), may hold values from -6 to 6
- pre_act: bfloat16 [32, 16, 64, 256], P('slab', 'filt'), may hold values from -6 to 6
- layer_input: bfloat16 [32, 16, 64, 128], P('slab', 'filt'), may hold values from -6 to 6
- weight_one: bfloat16 [27, 128, 256], replicated, may hold values from -0.078125 to 0.078125
- weight_two: bfloat16 [27, 256, 256], P(None, None, 'filt'), may hold values from -0.078125 to 0.078125
Outputs:
- grad_w2: float32 [27, 256, 256], P(None, None, 'filt')
- grad_w1: float32 [27, 128, 256], replicated
- grad_x0: bfloat16 [32, 16, 64, 128], P('slab', 'filt')
The draws below stay inside these ranges and needn't reach their ends.
All inputs are finite; a program needn't handle non-finite values.
Results may differ from the reference program's by a relative error of at most 0.0013.
Values may be sent and summed in bfloat16 or wider, within the bound.
No kernel may reach another device: no remote copies, remote signals or barrier semaphores. Data moves between devices by JAX's collectives and lax.ppermute only.
A program may use at most 128 MiB of HBM per device.

```python
import math
import jax
import jax.numpy as jnp
from jax import lax

CH_IN = 128
CH_MID = 256
CH_OUT = 256
ROWS = 16
COLS = 64
DEPTH = 32


def block_scale(key, dims, cuts, low, top_value):
    gain, own = 1.0, jax.random.fold_in(key, 6)
    for dim, shards_of in cuts:
        draws = jnp.exp(jax.random.uniform(jax.random.fold_in(own, dim), (shards_of,), jnp.float32, low / len(cuts), top_value / len(cuts)))
        gain = gain * jnp.repeat(draws, dims[dim] // shards_of).reshape([-1 if axis == dim else 1 for axis in range(len(dims))])
    return gain


def gaussian(rng, shape, deviation, most, cuts=(), dtype=jnp.bfloat16):
    level = block_scale(rng, shape, cuts, -0.22, 0.18) if cuts else 1.0
    values = jax.random.normal(rng, shape, jnp.float32) * deviation * level
    return jnp.minimum(jnp.maximum(values, -most), most).astype(dtype)


def setup_inputs(seed: int = 0) -> dict:
    streams_of = jax.random.split(jax.random.key(seed), 6)
    cotangent = gaussian(streams_of[0], (DEPTH, ROWS, COLS, CH_OUT), 1.0, 6.0, ((0, 16), (3, 16)))
    pre_act = gaussian(streams_of[1], (DEPTH, ROWS, COLS, CH_MID), 1.0, 6.0, ((0, 16), (1, 16)))
    layer_input = gaussian(streams_of[2], (DEPTH, ROWS, COLS, CH_IN), 1.0, 6.0, ((0, 16), (1, 16)))
    weight_one = gaussian(streams_of[3], (27, CH_IN, CH_MID), (27 * CH_MID) ** -0.5, 0.078125)
    weight_two = gaussian(streams_of[4], (27, CH_MID, CH_OUT), (27 * CH_OUT) ** -0.5, 0.078125, ((2, 16),))
    return {"cotangent": cotangent, "pre_act": pre_act, "layer_input": layer_input, "weight_one": weight_one, "weight_two": weight_two}


leak_slope = 0.3

def tap_offsets():
    return [(a, b, c) for a in (-1, 0, 1) for b in (-1, 0, 1) for c in (-1, 0, 1)]

def leaky_relu(value):
    return jnp.where(value > 0, value, leak_slope * value)

def relu_slope(value):
    return jnp.where(value > 0, jnp.float32(1.0), jnp.float32(leak_slope))

def pad_grid(field):
    return jnp.pad(field, ((1, 1), (1, 1), (1, 1), (0, 0)))

def filter_grad(source, signal, grad_scale):
    planes_here, row_count, col_count = signal.shape[:3]
    framed = pad_grid(source.astype(jnp.float32))
    flat_signal = signal.astype(jnp.float32).reshape(-1, signal.shape[3])
    results = []
    for a, b, c in tap_offsets():
        window_piece = framed[1 + a:1 + a + planes_here, 1 + b:1 + b + row_count, 1 + c:1 + c + col_count]
        window_piece = window_piece.reshape(-1, source.shape[3])
        results.append(jnp.dot(window_piece.T, flat_signal, preferred_element_type=jnp.float32, precision=lax.Precision.HIGHEST))
    return jnp.stack(results) * grad_scale

def data_grad(signal, weights):
    planes_here, row_count, col_count = signal.shape[:3]
    framed = pad_grid(signal.astype(jnp.float32))
    weights_wide = weights.astype(jnp.float32)
    back_sum = jnp.zeros((planes_here * row_count * col_count, weights.shape[1]), jnp.float32)
    for tap, (a, b, c) in enumerate(tap_offsets()):
        window_piece = framed[1 - a:1 - a + planes_here, 1 - b:1 - b + row_count, 1 - c:1 - c + col_count]
        window_piece = window_piece.reshape(-1, signal.shape[3])
        back_sum = back_sum + jnp.dot(window_piece, weights_wide[tap].T, preferred_element_type=jnp.float32, precision=lax.Precision.HIGHEST)
    return back_sum.reshape(planes_here, row_count, col_count, weights.shape[1])

def reference(cotangent, pre_act, layer_input, weight_one, weight_two):
    planes_here, row_count, col_count = cotangent.shape[:3]
    grad_scale = jnp.float32(1.0 / math.sqrt(planes_here * row_count * col_count))
    activation = leaky_relu(pre_act.astype(jnp.float32)).astype(jnp.bfloat16)
    grad_w2 = filter_grad(activation, cotangent, grad_scale)
    back_sum = data_grad(cotangent, weight_two)
    error_signal = back_sum * relu_slope(pre_act.astype(jnp.float32))
    grad_w1 = filter_grad(layer_input, error_signal, grad_scale)
    grad_x0 = data_grad(error_signal, weight_one).astype(jnp.bfloat16)
    return (grad_w2, grad_w1, grad_x0)
```

```python
import functools
import math

import jax
import jax.numpy as jnp
from jax import lax
from jax.experimental import pallas as pl
from jax.experimental.pallas import tpu as pltpu
from jax.sharding import PartitionSpec as P

leak_slope = 0.3
bf16 = jnp.bfloat16
f32 = jnp.float32
f16 = jnp.float16
top = 13.0
planes, rows, cols = 2, 16, 64
lanes = planes * cols
voxels = rows * lanes
block = 16
taps = 27

same_core = [[2 * i + core for i in range(8)] for core in range(2)]
core_swap = [(i, i ^ 1) for i in range(16)]
swaps = (2, 4, 12, 1)
block_order = [0]
for swap in swaps:
    block_order += [other ^ swap for other in block_order]
slab_up = [(i, i + 1) for i in range(15)]
slab_down = [(i + 1, i) for i in range(15)]


def params():
    return pltpu.CompilerParams(vmem_limit_bytes=48 * 1024 * 1024)


def cost(flops, moved):
    return pl.CostEstimate(flops=flops, bytes_accessed=moved, transcendentals=0)


def shape(dims, dtype):
    return jax.ShapeDtypeStruct(dims, dtype)


def whole(count):
    return [pl.BlockSpec(memory_space=pltpu.VMEM)] * count


def scalar_spec():
    return pl.BlockSpec(memory_space=pltpu.SMEM)


def exponent(value):
    most = jnp.max(jnp.max(jnp.abs(value), axis=0, keepdims=True), axis=1, keepdims=True)
    return jnp.ceil(jnp.log2(jnp.maximum(most, 2.0**-100)))


def weight_kernel(place, weight, own, sent):
    flat = weight[...].astype(f32).reshape(taps * block, 256).T.astype(bf16)
    low, high = flat[:128], flat[128:]
    own[...] = jnp.where(place[0] == 0, low, high)
    sent[...] = jnp.where(place[0] == 0, high, low)


def pack_kernel(cot, x, low, high):
    for plane, out in ((0, low), (1, high)):
        field = cot[plane].reshape(rows * block, cols)
        piece = x[plane]
        side = jnp.concatenate(
            [piece[:, :cols], piece[:, cols:], jnp.zeros((2 * cols, cols), bf16)], axis=0
        )
        out[...] = jnp.concatenate([field, side], axis=1)


def message_kernel(pre, x, packed, out):
    value = pre[...].astype(f32).reshape(lanes, 256)
    active = jnp.where(value > 0, value, leak_slope * value).astype(bf16)
    own = x[...].reshape(lanes, 128)
    for i in range(8):
        out[i, 0] = active[:, :128]
        out[i, 1] = active[:, 128:]
        out[i, 2] = own


def shifted_rows(field, b):
    gap = jnp.zeros((field.shape[0], lanes), field.dtype)
    if b == 1:
        return jnp.concatenate([gap, field[:, :-lanes]], axis=1)
    if b == -1:
        return jnp.concatenate([field[:, lanes:], gap], axis=1)
    return field


def shifted_columns(field, c):
    if c == 0:
        return field
    width = field.shape[1]
    col = lax.broadcasted_iota(jnp.int32, field.shape, 1) % cols
    edge = 0 if c == 1 else cols - 1
    return jnp.where(col == edge, jnp.zeros_like(field), pltpu.roll(field, c % width, axis=1))


def fill_columns(own, low, high, out):
    below = low[:, :cols].reshape(rows, block, cols)
    above = high[:, :cols].reshape(rows, block, cols)
    parts = [below, own[0], own[1], above]
    for a in (-1, 0, 1):
        pieces = []
        for r in range(rows):
            pieces += [parts[1 - a][r].astype(f32), parts[2 - a][r].astype(f32)]
        field = jnp.concatenate(
            [jnp.concatenate(pieces[2 * r : 2 * r + 2], axis=1) for r in range(rows)], axis=1
        )
        for c in (-1, 0, 1):
            moved = shifted_columns(field, c).astype(bf16)
            for b in (-1, 0, 1):
                tap = 9 * (a + 1) + 3 * (b + 1) + c + 1
                out[tap * block : (tap + 1) * block, :] = shifted_rows(moved, b)


def back_kernel(own, other, own_low, own_high, other_low, other_high, own_w, other_w, out, cot_cols, other_cols):
    fill_columns(own, own_low, own_high, cot_cols)
    fill_columns(other, other_low, other_high, other_cols)
    total = jnp.dot(own_w[...], cot_cols[...], preferred_element_type=f32)
    total += jnp.dot(other_w[...], other_cols[...], preferred_element_type=f32)
    power = exponent(total)
    out[:, :, :voxels] = (total * jnp.exp2(top - power)).reshape(8, block, voxels)
    rims = [
        jnp.concatenate([pack[0:cols, cols:], pack[cols : 2 * cols, cols:]], axis=1)
        for pack in (own_low, own_high)
    ]
    rim = jnp.concatenate(rims, axis=0).astype(f32)
    rim_power = exponent(rim)
    rim = rim * jnp.exp2(top - rim_power)
    side = [
        jnp.broadcast_to(power, (block, cols)),
        jnp.broadcast_to(rim_power, (block, cols)),
    ] + [rim[g * block : (g + 1) * block] for g in range(8)]
    side = jnp.concatenate(side, axis=1)
    for i in range(8):
        out[i, :, voxels:] = side


def second_kernel(place, cot_cols, own, other, grad, slope, active):
    core = place[0]
    first = place[0] * 128 + place[1] // 2 * block
    for i in range(8):
        for part, side in ((own, core), (other, 1 - core)):
            here = pl.ds(pl.multiple_of((2 * i + side) * lanes, lanes), lanes)
            active[here, 0:128] = part[i, 0]
            active[here, 128:256] = part[i, 1]
    grad[...] = jnp.dot(cot_cols[...], active[...], preferred_element_type=f32)
    positive = jnp.where(active[...].astype(f32) > 0, 1.0, 0.0).astype(bf16)
    mid = lax.broadcasted_iota(jnp.int32, (block, 256), 1)
    row = lax.broadcasted_iota(jnp.int32, (block, 256), 0)
    pick = jnp.where(mid == row + first, 1.0, 0.0).astype(bf16)
    mask = lax.dot_general(pick, positive, (((1,), (1,)), ((), ())), preferred_element_type=f32)
    slope[...] = jnp.where(mask > 0.5, 1.0, leak_slope)


def inputs_kernel(place, own, other, own_rims, other_rims, inputs):
    core = place[0]
    for i in range(8):
        for part, rims, at, side in ((own, own_rims, voxels, core), (other, other_rims, 0, 1 - core)):
            here = pl.ds(pl.multiple_of((2 * i + side) * lanes, lanes), lanes)
            middle = part[i, 2]
            scale = jnp.exp2(rims[i, 0:1, at + cols : at + cols + 1] - top)
            at += 128
            rim = [rims[i, :, at + g * 128 : at + (g + 1) * 128] for g in range(8)]
            rim = (jnp.concatenate(rim, axis=0) * scale).astype(bf16)
            inputs[here, 0:128] = jnp.concatenate([rim[:cols], middle[:cols]], axis=0)
            inputs[here, 128:256] = middle
            inputs[here, 256:384] = jnp.concatenate([middle[cols:], rim[cols:]], axis=0)


def split(value):
    high = value.astype(bf16)
    return high, (value - high.astype(f32)).astype(bf16)


def first_kernel(parts, slope, inputs, second, out, error, shifted):
    total = jnp.zeros((block, voxels), f32)
    for i in range(8):
        total = total + parts[i, :, :voxels] * jnp.exp2(parts[i, :, voxels : voxels + 1] - top)
    total = total * slope[...]
    error_power = exponent(total)
    error[:, :voxels] = total * jnp.exp2(top - error_power)
    error[:, voxels:] = jnp.broadcast_to(error_power, (block, 128))
    for c in (-1, 0, 1):
        pair = split(shifted_columns(total, c))
        for b in (-1, 0, 1):
            at = (3 * (b + 1) + c + 1) * 2 * block
            for k in range(2):
                shifted[at + k * block : at + (k + 1) * block, :] = shifted_rows(pair[k], b)
    grad = jnp.dot(shifted[...], inputs[...], preferred_element_type=f32)
    grad = grad.reshape(9, 2, block, 384)
    grad = grad[:, 0] + grad[:, 1]
    power = exponent(grad.reshape(9 * block, 384))
    grad = grad * jnp.exp2(top - power).reshape(1, 1, 1)
    for a in range(3):
        for bc in range(9):
            tap = 9 * a + bc
            out[tap * block : (tap + 1) * block, 0:128] = grad[bc, :, a * 128 : (a + 1) * 128]
    second_power = exponent(second[...])
    out[0 : taps * block, 128:384] = second[...] * jnp.exp2(top - second_power)
    out[taps * block :, 0:384] = jnp.zeros((5 * block, 384), f32)
    out[:, 384:448] = jnp.broadcast_to(power, (32 * block, cols))
    out[:, 448:512] = jnp.broadcast_to(second_power, (32 * block, cols))


def sum_kernel(place, sums, out, second_power):
    power = jnp.max(sums[:, :, 384:512], axis=0)
    low, high = power[:, 0:1], power[:, cols : cols + 1]
    first = jnp.zeros((2 * block, 128), f32)
    second = jnp.zeros((2 * block, 256), f32)
    for i in range(16):
        first += sums[i, :, 0:128] * jnp.exp2(sums[i, :, 384:385] - low - 4.0)
        second += sums[i, :, 128:384] * jnp.exp2(sums[i, :, 448:449] - high - 4.0)
    row = lax.broadcasted_iota(jnp.int32, (2 * block, 128), 0)
    keep = jnp.logical_or(place[2] != 13, row < block)
    out[:, 0:128] = jnp.where(keep, first, low + 4.0)
    out[:, 128:384] = second
    second_power[...] = jnp.broadcast_to(high[0:8] + 4.0, (8, 128))


def second_scale_kernel(grad_scale, grad, power, out):
    scale = jnp.exp2(power[0:1, 0:1] - top) * grad_scale
    out[...] = grad[...] * scale.reshape(1, 1, 1)


def input_kernel(place, blocks, weight, middle, to_low, to_high, field):
    filt = place[1]
    for j, other in enumerate(block_order):
        source = filt ^ other
        here = pl.ds(pl.multiple_of((source % 2 * 8 + source // 2) * block, block), block)
        scale = jnp.exp2(blocks[j, 0:1, voxels : voxels + 1] - top)
        for b in range(3):
            row = filt + b - 1
            at = pl.multiple_of(jnp.clip(row, 0, rows - 1) * lanes, lanes)
            inside = jnp.logical_and(row >= 0, row < rows)
            piece = jnp.where(inside, blocks[j, :, pl.ds(at, lanes)] * scale, 0.0)
            field[here, b * lanes : (b + 1) * lanes] = piece
    field = field[...]
    total = jnp.zeros((3 * 128, 2 * lanes), f32)
    for c in (-1, 0, 1):
        pair = split(shifted_columns(field, c))
        for b in (-1, 0, 1):
            at = (1 - b) * lanes
            window = jnp.concatenate([half[:, at : at + lanes] for half in pair], axis=1)
            tap = 3 * (b + 1) + c + 1
            taken = jnp.concatenate([weight[9 * a + tap] for a in range(3)], axis=0)
            total += jnp.dot(taken, window, preferred_element_type=f32)
    total = (total[:, :lanes] + total[:, lanes:]).T
    back, here, ahead = total[:, :128], total[:, 128:256], total[:, 256:]
    to_low[...] = back[:cols]
    to_high[...] = ahead[cols:]
    middle[0:cols] = here[:cols] + back[cols:]
    middle[cols:] = here[cols:] + ahead[:cols]


def rim_kernel(middle, low, high, out):
    out[0:cols] = (middle[0:cols] + low[...]).astype(bf16)
    out[cols:] = (middle[cols:] + high[...]).astype(bf16)


def gather_kernel(grad_scale, place, part, power, *rest):
    out = rest[-1]
    scale = jnp.exp2(power[...].reshape(128, 128) - top) * grad_scale
    row = lax.broadcasted_iota(jnp.int32, (128, 256), 0)
    lane = lax.broadcasted_iota(jnp.int32, (128, 256), 1) % 128
    unit = jnp.where(row == lane, 1.0, 0.0).astype(bf16)
    for t in range(9):
        value = part[:, t * block : (t + 1) * block].reshape(128, 128) * scale
        out[t] = lax.dot_general(
            unit,
            jnp.concatenate(split(value), axis=1),
            (((1,), (1,)), ((), ())),
            preferred_element_type=f32,
        )


def gather(grad_scale, place, wide, swapped, result):
    def half(i, place):
        return (i, 0, 1 - place[0] if swapped else place[0])

    extra = [] if result is None else [result]
    return pl.pallas_call(
        functools.partial(gather_kernel, grad_scale),
        out_shape=shape((taps, 128, 256), f32),
        grid_spec=pltpu.PrefetchScalarGridSpec(
            num_scalar_prefetch=1,
            grid=(3,),
            in_specs=[
                pl.BlockSpec((8, 9 * block, 128), lambda i, place: (0, i, 0)),
                pl.BlockSpec((8, block, 128), lambda i, place: (0, taps, 0)),
            ]
            + [pl.BlockSpec(memory_space=pl.ANY)] * len(extra),
            out_specs=pl.BlockSpec((9, 128, 128), half),
        ),
        input_output_aliases={3: 0} if extra else {},
        compiler_params=params(),
        cost_estimate=cost(2 * 128 * 128 * 256 * taps, 4 << 20),
        name="gather_other" if swapped else "gather_own",
    )(place, wide, wide, *extra)


def shards(cotangent, pre_act, layer_input, weight_one, weight_two):
    grad_scale = 1.0 / math.sqrt(voxels * 16)
    filt = lax.axis_index("filt")
    core = filt % 2
    place = jnp.stack([core, filt, lax.axis_index("slab")]).astype(jnp.int32)

    cot = cotangent.transpose(0, 1, 3, 2)
    x = layer_input.reshape(planes, cols, 128)
    pre = pre_act.reshape(planes, cols, 256)
    to_low, to_high = pl.pallas_call(
        pack_kernel,
        out_shape=[shape((256, 128), bf16)] * 2,
        in_specs=whole(2),
        out_specs=whole(2),
        compiler_params=params(),
        name="pack",
    )(cot, x)
    low = lax.ppermute(to_high, "slab", slab_up)
    high = lax.ppermute(to_low, "slab", slab_down)
    message = pl.pallas_call(
        message_kernel,
        out_shape=shape((8, 3, 128, 128), bf16),
        in_specs=whole(2) + [pl.BlockSpec(memory_space=pl.ANY)],
        out_specs=whole(1)[0],
        compiler_params=params(),
        name="message",
    )(pre, x, to_low)
    own_rows = lax.all_to_all(
        message, "filt", split_axis=0, concat_axis=0, tiled=True, axis_index_groups=same_core
    )
    other = lax.ppermute(cot, "filt", core_swap)
    own_w, sent_w = pl.pallas_call(
        weight_kernel,
        out_shape=[shape((128, taps * block), bf16)] * 2,
        in_specs=[scalar_spec()] + whole(1),
        out_specs=whole(2),
        compiler_params=params(),
        name="weights",
    )(place, weight_two.transpose(0, 2, 1))
    other_w = lax.ppermute(sent_w, "filt", core_swap)
    other_low = lax.ppermute(low, "filt", core_swap)
    other_high = lax.ppermute(high, "filt", core_swap)

    partial, cot_cols = pl.pallas_call(
        back_kernel,
        out_shape=[shape((8, block, voxels + 1152), f32), shape((taps * block, voxels), bf16)],
        in_specs=whole(8),
        out_specs=whole(2),
        scratch_shapes=[pltpu.VMEM((taps * block, voxels), bf16)],
        compiler_params=params(),
        cost_estimate=cost(2 * 864 * 128 * 2048, 4 << 20),
        name="back",
    )(cot, other, low, high, other_low, other_high, own_w, other_w)
    partial = partial.astype(f16)
    own_rows, _ = lax.optimization_barrier((own_rows, partial))
    parts = lax.all_to_all(
        partial, "filt", split_axis=0, concat_axis=0, tiled=True, axis_index_groups=same_core
    )
    other_rows = lax.ppermute(own_rows, "filt", core_swap)
    second, slope = pl.pallas_call(
        second_kernel,
        out_shape=[shape((taps * block, 256), f32), shape((block, voxels), f32)],
        in_specs=[scalar_spec()] + whole(3),
        out_specs=whole(2),
        scratch_shapes=[pltpu.VMEM((voxels, 256), bf16)],
        compiler_params=params(),
        cost_estimate=cost(2 * 432 * 2048 * 256, 6 << 20),
        name="second",
    )(place, cot_cols, own_rows, other_rows)
    parts, _ = lax.optimization_barrier((parts, second))
    other_rims = lax.ppermute(parts[:, :, voxels:], "filt", core_swap).astype(f32)
    parts = parts.astype(f32)
    inputs = pl.pallas_call(
        inputs_kernel,
        out_shape=shape((voxels, 384), bf16),
        in_specs=[scalar_spec()] + whole(4),
        out_specs=whole(1)[0],
        compiler_params=params(),
        name="inputs",
    )(place, own_rows, other_rows, parts, other_rims)

    merged, error = pl.pallas_call(
        first_kernel,
        out_shape=[shape((512, 512), f32), shape((block, voxels + 128), f32)],
        in_specs=whole(4),
        out_specs=whole(2),
        scratch_shapes=[pltpu.VMEM((18 * block, voxels), bf16)],
        compiler_params=params(),
        cost_estimate=cost(2 * 288 * 2048 * 384, 6 << 20),
        name="first",
    )(parts, slope, inputs, second)

    sums = lax.all_to_all(
        merged.reshape(16, 32, 512).astype(f16), "slab", split_axis=0, concat_axis=0, tiled=True
    )
    blocks = error.astype(f16)[None]
    steps = []
    for swap in swaps:
        arrived = lax.ppermute(blocks, "filt", [(i, i ^ swap) for i in range(16)])
        blocks = jnp.concatenate([blocks, arrived], axis=0)
        steps.append(blocks)
    middle, rim_low, rim_high = pl.pallas_call(
        input_kernel,
        out_shape=[shape((lanes, 128), f32)] + [shape((cols, 128), f32)] * 2,
        in_specs=[scalar_spec()] + whole(2),
        out_specs=whole(3),
        scratch_shapes=[pltpu.VMEM((256, 3 * lanes), f32)],
        compiler_params=params(),
        cost_estimate=cost(2 * 128 * 256 * 256 * taps, 4 << 20),
        name="input",
    )(place, blocks.astype(f32), weight_one)
    rim_low, rim_high = (
        lax.ppermute(rim_high, "slab", slab_up),
        lax.ppermute(rim_low, "slab", slab_down),
    )
    grad_x0 = pl.pallas_call(
        rim_kernel,
        out_shape=shape((lanes, 128), bf16),
        in_specs=whole(3),
        out_specs=whole(1)[0],
        compiler_params=params(),
        name="rim",
    )(middle, rim_low, rim_high).reshape(planes, 1, cols, 128)
    sums, _ = lax.optimization_barrier((sums, steps[1]))
    mine, second_power = pl.pallas_call(
        sum_kernel,
        out_shape=[shape((32, 384), f32), shape((8, 128), f32)],
        in_specs=[scalar_spec()] + whole(1),
        out_specs=whole(2),
        compiler_params=params(),
        name="sum",
    )(place, sums.astype(f32))
    near = jnp.broadcast_to(mine.astype(f16)[None], (16, 32, 384))
    near = lax.all_to_all(near, "slab", split_axis=0, concat_axis=0, tiled=True)
    near, _ = lax.optimization_barrier((near, middle))
    near = near.reshape(32, block, 384)
    wide = jnp.broadcast_to(near[None, :28, :, :128], (8, 28, block, 128))
    wide = wide.reshape(8, 28 * block, 128)
    wide = lax.all_to_all(
        wide, "filt", split_axis=0, concat_axis=0, tiled=True, axis_index_groups=same_core
    )
    grad_w2 = pl.pallas_call(
        functools.partial(second_scale_kernel, grad_scale),
        out_shape=shape((taps, block, 256), f32),
        in_specs=whole(2),
        out_specs=whole(1)[0],
        compiler_params=params(),
        name="second_scale",
    )(near[:taps, :, 128:].astype(f32), second_power).transpose(0, 2, 1)
    wide, grad_w2, grad_x0 = lax.optimization_barrier((wide, grad_w2, grad_x0))
    other_wide = lax.ppermute(wide, "filt", core_swap)
    grad_w1 = gather(grad_scale, place, wide.astype(f32), False, None)
    grad_w1 = gather(grad_scale, place, other_wide.astype(f32), True, grad_w1)
    return (grad_w2, grad_w1, grad_x0)


def solution(mesh):
    return jax.shard_map(
        shards,
        mesh=mesh,
        in_specs=(
            P("slab", None, None, "filt"),
            P("slab", "filt", None, None),
            P("slab", "filt", None, None),
            P(),
            P(None, None, "filt"),
        ),
        out_specs=(P(None, None, "filt"), P(), P("slab", "filt", None, None)),
        check_vma=False,
    )
```

```python
import functools
import math

import jax
import jax.numpy as jnp
from jax import lax
from jax.experimental import pallas as pl
from jax.experimental.pallas import tpu as pltpu
from jax.sharding import PartitionSpec as P

leak_slope = 0.3
bf16 = jnp.bfloat16
f32 = jnp.float32
f16 = jnp.float16
top = 13.0
planes, rows, cols = 2, 16, 64
lanes = planes * cols
voxels = rows * lanes
block = 16
taps = 27

same_core = [[2 * i + core for i in range(8)] for core in range(2)]
z_swap = [(i, i ^ 2) for i in range(16)]
core_swap = [(i, i ^ 1) for i in range(16)]
share = 88
swaps = ((4,), (12,), (1,))
block_order = [0]
for together in swaps:
    block_order += [other ^ swap for swap in together for other in block_order]
slab_step = [(s * 16 + f, (s + 1) * 16 + f) for s in range(15) for f in range(0, 16, 2)]
slab_step += [((s + 1) * 16 + f, s * 16 + f) for s in range(15) for f in range(1, 16, 2)]


def params():
    return pltpu.CompilerParams(vmem_limit_bytes=48 * 1024 * 1024)


def cost(flops, moved):
    return pl.CostEstimate(flops=flops, bytes_accessed=moved, transcendentals=0)


def shape(dims, dtype):
    return jax.ShapeDtypeStruct(dims, dtype)


def whole(count):
    return [pl.BlockSpec(memory_space=pltpu.VMEM)] * count


def scalar_spec():
    return pl.BlockSpec(memory_space=pltpu.SMEM)


def exponent(value):
    most = jnp.max(jnp.max(jnp.abs(value), axis=0, keepdims=True), axis=1, keepdims=True)
    return jnp.ceil(jnp.log2(jnp.maximum(most, 2.0**-100)))


def weight_kernel(place, weight, ready, own, sent):
    flat = weight[...].astype(f32).reshape(taps * block, 256).T.astype(bf16)
    low, high = flat[:128], flat[128:]
    own[...] = jnp.where(place[0] == 0, low, high)
    sent[...] = jnp.where(place[0] == 0, high, low)


def pack_kernel(place, cot, x, keep, swap):
    core = place[0]
    for plane, out in ((1 - core, keep), (core, swap)):
        field = cot[plane].reshape(rows * block, cols)
        piece = x[plane]
        side = jnp.concatenate(
            [piece[:, :cols], piece[:, cols:], jnp.zeros((2 * cols, cols), bf16)], axis=0
        )
        out[...] = jnp.concatenate([field, side], axis=1)


def message_kernel(pre, x, packed, out):
    value = pre[...].astype(f32).reshape(lanes, 256)
    active = jnp.where(value > 0, value, leak_slope * value).astype(bf16)
    own = x[...].reshape(lanes, 128)
    for i in range(8):
        out[i, 0] = active[:, :128]
        out[i, 1] = active[:, 128:]
        out[i, 2] = own


def shifted_rows(field, b):
    gap = jnp.zeros((field.shape[0], lanes), field.dtype)
    if b == 1:
        return jnp.concatenate([gap, field[:, :-lanes]], axis=1)
    if b == -1:
        return jnp.concatenate([field[:, lanes:], gap], axis=1)
    return field


def shifted_columns(field, c):
    if c == 0:
        return field
    width = field.shape[1]
    col = lax.broadcasted_iota(jnp.int32, field.shape, 1) % cols
    edge = 0 if c == 1 else cols - 1
    return jnp.where(col == edge, jnp.zeros_like(field), pltpu.roll(field, c % width, axis=1))


def fill_columns(own, low, high, out):
    below = low[:, :cols].reshape(rows, block, cols)
    above = high[:, :cols].reshape(rows, block, cols)
    parts = [below, own[0], own[1], above]
    for a in (-1, 0, 1):
        pieces = []
        for r in range(rows):
            pieces += [parts[1 - a][r].astype(f32), parts[2 - a][r].astype(f32)]
        field = jnp.concatenate(
            [jnp.concatenate(pieces[2 * r : 2 * r + 2], axis=1) for r in range(rows)], axis=1
        )
        for c in (-1, 0, 1):
            moved = shifted_columns(field, c).astype(bf16)
            for b in (-1, 0, 1):
                tap = 9 * (a + 1) + 3 * (b + 1) + c + 1
                out[tap * block : (tap + 1) * block, :] = shifted_rows(moved, b)


def back_kernel(place, own, other, here, there, own_w, other_w, out, cot_cols, other_cols):
    core = place[0]
    own_low, own_high = (jnp.where(core == side, here[0], there[1]) for side in range(2))
    other_low, other_high = (jnp.where(core == side, here[1], there[0]) for side in range(2))
    fill_columns(own, own_low, own_high, cot_cols)
    fill_columns(other, other_low, other_high, other_cols)
    total = jnp.dot(own_w[...], cot_cols[...], preferred_element_type=f32)
    total += jnp.dot(other_w[...], other_cols[...], preferred_element_type=f32)
    power = exponent(total)
    out[:, :, :voxels] = (total * jnp.exp2(top - power)).reshape(8, block, voxels)
    rims = [
        jnp.concatenate([pack[0:cols, cols:], pack[cols : 2 * cols, cols:]], axis=1)
        for pack in (own_low, own_high)
    ]
    rim = jnp.concatenate(rims, axis=0).astype(f32)
    rim_power = exponent(rim)
    rim = rim * jnp.exp2(top - rim_power)
    side = [
        jnp.broadcast_to(power, (block, cols)),
        jnp.broadcast_to(rim_power, (block, cols)),
    ] + [rim[g * block : (g + 1) * block] for g in range(8)]
    side = jnp.concatenate(side, axis=1)
    for i in range(8):
        out[i, :, voxels:] = side


def second_kernel(place, cot_cols, own, other, grad, slope, active):
    core = place[0]
    first = place[0] * 128 + place[1] // 2 * block
    for i in range(8):
        for part, side in ((own, core), (other, 1 - core)):
            here = pl.ds(pl.multiple_of((2 * i + side) * lanes, lanes), lanes)
            active[here, 0:128] = part[i, 0]
            active[here, 128:256] = part[i, 1]
    grad[...] = jnp.dot(cot_cols[...], active[...], preferred_element_type=f32)
    positive = jnp.where(active[...].astype(f32) > 0, 1.0, 0.0).astype(bf16)
    mid = lax.broadcasted_iota(jnp.int32, (block, 256), 1)
    row = lax.broadcasted_iota(jnp.int32, (block, 256), 0)
    pick = jnp.where(mid == row + first, 1.0, 0.0).astype(bf16)
    mask = lax.dot_general(pick, positive, (((1,), (1,)), ((), ())), preferred_element_type=f32)
    slope[...] = jnp.where(mask > 0.5, 1.0, leak_slope)


def inputs_kernel(place, own, other, own_rims, other_rims, inputs):
    core = place[0]
    for i in range(8):
        for part, rims, at, side in ((own, own_rims, voxels, core), (other, other_rims, 0, 1 - core)):
            here = pl.ds(pl.multiple_of((2 * i + side) * lanes, lanes), lanes)
            middle = part[i, 2]
            scale = jnp.exp2(rims[i, 0:1, at + cols : at + cols + 1] - top)
            at += 128
            rim = [rims[i, :, at + g * 128 : at + (g + 1) * 128] for g in range(8)]
            rim = (jnp.concatenate(rim, axis=0) * scale).astype(bf16)
            inputs[here, 0:128] = jnp.concatenate([rim[:cols], middle[:cols]], axis=0)
            inputs[here, 128:256] = middle
            inputs[here, 256:384] = jnp.concatenate([middle[cols:], rim[cols:]], axis=0)


def split(value):
    high = value.astype(bf16)
    return high, (value - high.astype(f32)).astype(bf16)


def first_kernel(parts, slope, inputs, second, out, scaled, shifted):
    total = jnp.zeros((block, voxels), f32)
    for i in range(8):
        total = total + parts[i, :, :voxels] * jnp.exp2(parts[i, :, voxels : voxels + 1] - top)
    total = total * slope[...]
    power = exponent(total)
    scaled[:, :voxels] = total * jnp.exp2(top - power)
    scaled[:, voxels:] = jnp.broadcast_to(power, (block, 128))
    for c in (-1, 0, 1):
        pair = split(shifted_columns(total, c))
        for b in (-1, 0, 1):
            at = (3 * (b + 1) + c + 1) * 2 * block
            for k in range(2):
                shifted[at + k * block : at + (k + 1) * block, :] = shifted_rows(pair[k], b)
    grad = jnp.dot(shifted[...], inputs[...], preferred_element_type=f32)
    grad = grad.reshape(9, 2, block, 384)
    grad = grad[:, 0] + grad[:, 1]
    power = exponent(grad.reshape(9 * block, 384))
    grad = grad * jnp.exp2(top - power).reshape(1, 1, 1)
    second_power = exponent(second[...])
    other = second[...] * jnp.exp2(top - second_power)
    pieces = [grad[bc, :, a * 128 : (a + 1) * 128] for a in range(3) for bc in range(9)]
    pieces += [other[:, :128], other[:, 128:], jnp.zeros((share * 16 - 3 * taps * block, 128), f32)]
    flat = jnp.concatenate(pieces, axis=0)
    powers = jnp.concatenate(
        [jnp.broadcast_to(power, (8, cols)), jnp.broadcast_to(second_power, (8, cols))], axis=1
    )
    for i in range(16):
        out[i, :share] = flat[i * share : (i + 1) * share]
        out[i, share:] = powers


def sum_kernel(place, sums, out):
    power = jnp.max(sums[:, share:], axis=0)
    row = lax.broadcasted_iota(jnp.int32, (share, 1), 0) + place[2] * share
    total = jnp.zeros((share, 128), f32)
    for i in range(16):
        change = sums[i, share:] - power - 4.0
        scale = jnp.where(row < taps * block, change[0:1, 0:1], change[0:1, cols : cols + 1])
        total += sums[i, :share] * jnp.exp2(scale)
    out[:share] = total
    out[share:] = power + 4.0


def second_scale_kernel(grad_scale, grad, power, ready, out):
    scale = jnp.exp2(power[0:1, cols : cols + 1] - top) * grad_scale
    out[:, :, :128] = grad[0] * scale.reshape(1, 1, 1)
    out[:, :, 128:] = grad[1] * scale.reshape(1, 1, 1)


def input_kernel(place, blocks, weight, mine, theirs, field):
    filt = place[1]
    for target, out in ((filt, mine), (filt ^ 2, theirs)):
        field[...] = jnp.zeros((256, 3 * lanes), f32)
        for j, other in enumerate(block_order):
            source = filt ^ other
            here = pl.ds(pl.multiple_of((source % 2 * 8 + source // 2) * block, block), block)
            scale = jnp.exp2(blocks[j, 0:1, voxels : voxels + 1] - top)
            for b in range(3):
                row = target + b - 1
                at = pl.multiple_of(jnp.clip(row, 0, rows - 1) * lanes, lanes)
                inside = jnp.logical_and(row >= 0, row < rows)
                piece = jnp.where(inside, blocks[j, :, pl.ds(at, lanes)] * scale, 0.0)
                field[here, b * lanes : (b + 1) * lanes] = piece
        total = jnp.zeros((3 * 128, 2 * lanes), f32)
        for c in (-1, 0, 1):
            pair = split(shifted_columns(field[...], c))
            for b in (-1, 0, 1):
                at = (1 - b) * lanes
                window = jnp.concatenate([half[:, at : at + lanes] for half in pair], axis=1)
                tap = 3 * (b + 1) + c + 1
                taken = jnp.concatenate([weight[9 * a + tap] for a in range(3)], axis=0)
                total += jnp.dot(taken, window, preferred_element_type=f32)
        total = (total[:, :lanes] + total[:, lanes:]).T
        back, middle, ahead = total[:, :128], total[:, 128:256], total[:, 256:]
        out[0:cols] = middle[:cols] + back[cols:]
        out[cols:lanes] = middle[cols:] + ahead[:cols]
        out[lanes : 3 * cols] = back[:cols]
        out[3 * cols :] = ahead[cols:]


def edge_kernel(place, mine, arrived, middle, keep, swap):
    core = place[0]
    middle[...] = mine[0:lanes] + arrived[0:lanes]
    low = mine[lanes : 3 * cols] + arrived[lanes : 3 * cols]
    high = mine[3 * cols :] + arrived[3 * cols :]
    keep[...] = jnp.where(core == 0, high, low)
    swap[...] = jnp.where(core == 0, low, high)


def rim_kernel(place, middle, here, there, out):
    core = place[0]
    low, high = (jnp.where(core == side, here[0], there[...]) for side in range(2))
    out[0:cols] = (middle[0:cols] + low).astype(bf16)
    out[cols:] = (middle[cols:] + high).astype(bf16)


def gather_kernel(grad_scale, place, own, other, out):
    core = place[0]
    start = pl.program_id(0) * 9 * block
    for part, side in ((own, core), (other, 1 - core)):
        power = [
            jnp.broadcast_to(part[i, taps * block : taps * block + 1, 0:1], (block, 1))
            for i in range(8)
        ]
        scale = jnp.exp2(jnp.concatenate(power, axis=0) - top) * grad_scale
        half = pl.ds(pl.multiple_of(side * 128, 128), 128)
        for t in range(9):
            here = pl.ds(pl.multiple_of(start + t * block, block), block)
            out[t, :, half] = (part[:, here].reshape(128, 128) * scale).T


def shards(cotangent, pre_act, layer_input, weight_one, weight_two):
    grad_scale = 1.0 / math.sqrt(voxels * 16)
    filt = lax.axis_index("filt")
    core = filt % 2
    place = jnp.stack([core, filt, lax.axis_index("slab")]).astype(jnp.int32)

    cot = cotangent.transpose(0, 1, 3, 2)
    x = layer_input.reshape(planes, cols, 128)
    pre = pre_act.reshape(planes, cols, 256)
    keep, swap = pl.pallas_call(
        pack_kernel,
        out_shape=[shape((256, 128), bf16)] * 2,
        in_specs=[scalar_spec()] + [pl.BlockSpec()] * 2,
        out_specs=whole(2),
        compiler_params=params(),
        name="pack",
    )(place, cot, x)
    swapped = lax.ppermute(swap, "filt", core_swap)
    here = lax.ppermute(jnp.stack([keep, swapped]), ("slab", "filt"), slab_step)
    there = lax.ppermute(here, "filt", core_swap)
    message = pl.pallas_call(
        message_kernel,
        out_shape=shape((8, 3, 128, 128), bf16),
        in_specs=[pl.BlockSpec()] * 2 + [pl.BlockSpec(memory_space=pl.ANY)],
        out_specs=whole(1)[0],
        compiler_params=params(),
        name="message",
    )(pre, x, swap)
    own_rows = lax.all_to_all(
        message, "filt", split_axis=0, concat_axis=0, tiled=True, axis_index_groups=same_core
    )
    other = lax.ppermute(cot, "filt", core_swap)
    own_w, sent_w = pl.pallas_call(
        weight_kernel,
        out_shape=[shape((128, taps * block), bf16)] * 2,
        in_specs=[scalar_spec()] + [pl.BlockSpec()] + [pl.BlockSpec(memory_space=pl.ANY)],
        out_specs=whole(2),
        compiler_params=params(),
        cost_estimate=cost(12 * 10**9, 1 << 20),
        name="weights",
    )(place, weight_two.transpose(0, 2, 1), here)
    other_w = lax.ppermute(sent_w, "filt", core_swap)

    partial, cot_cols = pl.pallas_call(
        back_kernel,
        out_shape=[shape((8, block, voxels + 1152), f32), shape((taps * block, voxels), bf16)],
        in_specs=[scalar_spec()] + whole(6),
        out_specs=whole(2),
        scratch_shapes=[pltpu.VMEM((taps * block, voxels), bf16)],
        compiler_params=params(),
        cost_estimate=cost(10**10, 4 << 20),
        name="back",
    )(place, cot, other, here, there, own_w, other_w)
    partial = partial.astype(f16)
    own_rows, _ = lax.optimization_barrier((own_rows, partial))
    parts = lax.all_to_all(
        partial, "filt", split_axis=0, concat_axis=0, tiled=True, axis_index_groups=same_core
    )
    other_rows = lax.ppermute(own_rows, "filt", core_swap)
    second, slope = pl.pallas_call(
        second_kernel,
        out_shape=[shape((taps * block, 256), f32), shape((block, voxels), f32)],
        in_specs=[scalar_spec()] + whole(3),
        out_specs=whole(2),
        scratch_shapes=[pltpu.VMEM((voxels, 256), bf16)],
        compiler_params=params(),
        cost_estimate=cost(2 * 432 * 2048 * 256, 6 << 20),
        name="second",
    )(place, cot_cols, own_rows, other_rows)
    parts, _ = lax.optimization_barrier((parts, second))
    rims = parts[:, :, voxels:]
    other_rims = lax.ppermute(rims, "filt", core_swap).astype(f32)
    parts = parts.astype(f32)
    inputs = pl.pallas_call(
        inputs_kernel,
        out_shape=shape((voxels, 384), bf16),
        in_specs=[scalar_spec()] + whole(4),
        out_specs=whole(1)[0],
        compiler_params=params(),
        cost_estimate=cost(10**7, 1 << 20),
        name="inputs",
    )(place, own_rows, other_rows, parts, other_rims)

    merged, scaled = pl.pallas_call(
        first_kernel,
        out_shape=[shape((16, share + 8, 128), f32), shape((block, voxels + 128), f32)],
        in_specs=whole(4),
        out_specs=whole(2),
        scratch_shapes=[pltpu.VMEM((18 * block, voxels), bf16)],
        compiler_params=params(),
        cost_estimate=cost(2 * 288 * 2048 * 384, 6 << 20),
        name="first",
    )(parts, slope, inputs, second)
    merged = merged.astype(f16)
    sums = lax.all_to_all(merged, "slab", split_axis=0, concat_axis=0, tiled=True)

    blocks, _ = lax.optimization_barrier((scaled.astype(f16)[None], inputs))
    for together in swaps:
        arrived = [
            lax.ppermute(blocks, "filt", [(i, i ^ swap) for i in range(16)]) for swap in together
        ]
        blocks = jnp.concatenate([blocks] + arrived, axis=0)
    mine_x0, theirs_x0 = pl.pallas_call(
        input_kernel,
        out_shape=[shape((2 * lanes, 128), f32)] * 2,
        in_specs=[scalar_spec()] + whole(2),
        out_specs=whole(2),
        scratch_shapes=[pltpu.VMEM((256, 3 * lanes), f32)],
        compiler_params=params(),
        cost_estimate=cost(4 * 128 * 256 * 256 * taps, 4 << 20),
        name="input",
    )(place, blocks.astype(f32), weight_one)
    arrived_x0 = lax.ppermute(theirs_x0, "filt", z_swap)
    mine = pl.pallas_call(
        sum_kernel,
        out_shape=shape((share + 8, 128), f32),
        in_specs=[scalar_spec()] + whole(1),
        out_specs=whole(1)[0],
        compiler_params=params(),
        name="sum",
    )(place, sums.astype(f32))
    near = jnp.broadcast_to(mine.astype(f16)[None], (16, share + 8, 128))
    near = lax.all_to_all(near, "slab", split_axis=0, concat_axis=0, tiled=True)
    near, arrived_x0 = lax.optimization_barrier((near, arrived_x0))
    middle, keep, swap = pl.pallas_call(
        edge_kernel,
        out_shape=[shape((lanes, 128), f32)] + [shape((cols, 128), f32)] * 2,
        in_specs=[scalar_spec()] + whole(2),
        out_specs=whole(3),
        compiler_params=params(),
        name="edge",
    )(place, mine_x0, arrived_x0)
    swapped = lax.ppermute(swap, "filt", core_swap)
    rims = lax.ppermute(jnp.stack([keep, swapped]), ("slab", "filt"), slab_step)
    other_rim = lax.ppermute(rims[1], "filt", core_swap)
    grad_x0 = pl.pallas_call(
        rim_kernel,
        out_shape=shape((lanes, 128), bf16),
        in_specs=[scalar_spec()] + whole(3),
        out_specs=whole(1)[0],
        compiler_params=params(),
        name="rim",
    )(place, middle, rims, other_rim).reshape(planes, 1, cols, 128)
    flat = near[:, :share].reshape(16 * share, 128)
    power = near[0, share:]
    wide = jnp.concatenate([flat[: taps * block], power], axis=0)
    wide = jnp.broadcast_to(wide[None], (8, taps * block + 8, 128))
    wide = lax.all_to_all(
        wide, "filt", split_axis=0, concat_axis=0, tiled=True, axis_index_groups=same_core
    )
    wide, grad_x0 = lax.optimization_barrier((wide, grad_x0))
    other_wide = lax.ppermute(wide, "filt", core_swap)
    own_wide = wide.astype(f32)
    grad_w2 = pl.pallas_call(
        functools.partial(second_scale_kernel, grad_scale),
        out_shape=shape((taps, block, 256), f32),
        in_specs=whole(2) + [pl.BlockSpec(memory_space=pl.ANY)],
        out_specs=whole(1)[0],
        compiler_params=params(),
        cost_estimate=cost(5 * 10**9, 1 << 20),
        name="second_scale",
    )(
        flat[taps * block : 3 * taps * block].reshape(2, taps, block, 128).astype(f32),
        power.astype(f32),
        own_wide,
    ).transpose(0, 2, 1)
    grad_w1 = pl.pallas_call(
        functools.partial(gather_kernel, grad_scale),
        out_shape=shape((taps, 128, 256), f32),
        grid=(3,),
        in_specs=[scalar_spec()] + whole(2),
        out_specs=pl.BlockSpec((9, 128, 256), lambda i: (i, 0, 0)),
        compiler_params=params(),
        name="gather",
    )(place, own_wide, other_wide.astype(f32))
    return (grad_w2, grad_w1, grad_x0)


def solution(mesh):
    return jax.shard_map(
        shards,
        mesh=mesh,
        in_specs=(
            P("slab", None, None, "filt"),
            P("slab", "filt", None, None),
            P("slab", "filt", None, None),
            P(),
            P(None, None, "filt"),
        ),
        out_specs=(P(None, None, "filt"), P(), P("slab", "filt", None, None)),
        check_vma=False,
    )
```

```python
import functools
import math

import jax
import jax.numpy as jnp
from jax import lax
from jax.experimental import pallas as pl
from jax.experimental.pallas import tpu as pltpu
from jax.sharding import PartitionSpec as P

leak_slope = 0.3
bf16 = jnp.bfloat16
f32 = jnp.float32
f16 = jnp.float16
top = 13.0
planes, rows, cols = 2, 16, 64
lanes = planes * cols
voxels = rows * lanes
block = 16
taps = 27

same_core = [[2 * i + core for i in range(8)] for core in range(2)]
z_swap = [(i, i ^ 2) for i in range(16)]
core_swap = [(i, i ^ 1) for i in range(16)]
share = 88
swaps = ((4,), (12,), (1,))
block_order = [0]
for together in swaps:
    block_order += [other ^ swap for swap in together for other in block_order]
slab_step = [(s * 16 + f, (s + 1) * 16 + f) for s in range(15) for f in range(0, 16, 2)]
slab_step += [((s + 1) * 16 + f, s * 16 + f) for s in range(15) for f in range(1, 16, 2)]


def params():
    return pltpu.CompilerParams(vmem_limit_bytes=48 * 1024 * 1024)


def cost(flops, moved):
    return pl.CostEstimate(flops=flops, bytes_accessed=moved, transcendentals=0)


def shape(dims, dtype):
    return jax.ShapeDtypeStruct(dims, dtype)


def whole(count):
    return [pl.BlockSpec(memory_space=pltpu.VMEM)] * count


def scalar_spec():
    return pl.BlockSpec(memory_space=pltpu.SMEM)


def exponent(value):
    most = jnp.max(jnp.max(jnp.abs(value), axis=0, keepdims=True), axis=1, keepdims=True)
    return jnp.ceil(jnp.log2(jnp.maximum(most, 2.0**-100)))


def weight_kernel(place, weight, ready, own, sent):
    flat = weight[...].astype(f32).reshape(taps * block, 256).T.astype(bf16)
    low, high = flat[:128], flat[128:]
    own[...] = jnp.where(place[0] == 0, low, high)
    sent[...] = jnp.where(place[0] == 0, high, low)


def pack_kernel(place, cot, x, keep, swap):
    core = place[0]
    for plane, out in ((1 - core, keep), (core, swap)):
        field = cot[plane].reshape(rows * block, cols)
        piece = x[plane]
        side = jnp.concatenate(
            [piece[:, :cols], piece[:, cols:], jnp.zeros((2 * cols, cols), bf16)], axis=0
        )
        out[...] = jnp.concatenate([field, side], axis=1)


def message_kernel(pre, x, packed, out):
    value = pre[...].astype(f32).reshape(lanes, 256)
    active = jnp.where(value > 0, value, leak_slope * value).astype(bf16)
    own = x[...].reshape(lanes, 128)
    for i in range(8):
        out[i, 0] = active[:, :128]
        out[i, 1] = active[:, 128:]
        out[i, 2] = own


def shifted_rows(field, b):
    gap = jnp.zeros((field.shape[0], lanes), field.dtype)
    if b == 1:
        return jnp.concatenate([gap, field[:, :-lanes]], axis=1)
    if b == -1:
        return jnp.concatenate([field[:, lanes:], gap], axis=1)
    return field


def shifted_columns(field, c):
    if c == 0:
        return field
    width = field.shape[1]
    col = lax.broadcasted_iota(jnp.int32, field.shape, 1) % cols
    edge = 0 if c == 1 else cols - 1
    return jnp.where(col == edge, jnp.zeros_like(field), pltpu.roll(field, c % width, axis=1))


def fill_columns(own, low, high, out):
    below = low[:, :cols].reshape(rows, block, cols)
    above = high[:, :cols].reshape(rows, block, cols)
    parts = [below, own[0], own[1], above]
    for a in (-1, 0, 1):
        pieces = []
        for r in range(rows):
            pieces += [parts[1 - a][r].astype(f32), parts[2 - a][r].astype(f32)]
        field = jnp.concatenate(
            [jnp.concatenate(pieces[2 * r : 2 * r + 2], axis=1) for r in range(rows)], axis=1
        )
        for c in (-1, 0, 1):
            moved = shifted_columns(field, c).astype(bf16)
            for b in (-1, 0, 1):
                tap = 9 * (a + 1) + 3 * (b + 1) + c + 1
                out[tap * block : (tap + 1) * block, :] = shifted_rows(moved, b)


def back_kernel(place, own, other, here, there, own_w, other_w, out, cot_cols, other_cols):
    core = place[0]
    own_low, own_high = (jnp.where(core == side, here[0], there[1]) for side in range(2))
    other_low, other_high = (jnp.where(core == side, here[1], there[0]) for side in range(2))
    fill_columns(own, own_low, own_high, cot_cols)
    fill_columns(other, other_low, other_high, other_cols)
    total = jnp.dot(own_w[...], cot_cols[...], preferred_element_type=f32)
    total += jnp.dot(other_w[...], other_cols[...], preferred_element_type=f32)
    power = exponent(total)
    out[:, :, :voxels] = (total * jnp.exp2(top - power)).reshape(8, block, voxels)
    rims = [
        jnp.concatenate([pack[0:cols, cols:], pack[cols : 2 * cols, cols:]], axis=1)
        for pack in (own_low, own_high)
    ]
    rim = jnp.concatenate(rims, axis=0).astype(f32)
    rim_power = exponent(rim)
    rim = rim * jnp.exp2(top - rim_power)
    side = [
        jnp.broadcast_to(power, (block, cols)),
        jnp.broadcast_to(rim_power, (block, cols)),
    ] + [rim[g * block : (g + 1) * block] for g in range(8)]
    side = jnp.concatenate(side, axis=1)
    for i in range(8):
        out[i, :, voxels:] = side


def second_kernel(place, cot_cols, own, other, grad, slope, active):
    core = place[0]
    first = place[0] * 128 + place[1] // 2 * block
    for i in range(8):
        for part, side in ((own, core), (other, 1 - core)):
            here = pl.ds(pl.multiple_of((2 * i + side) * lanes, lanes), lanes)
            active[here, 0:128] = part[i, 0]
            active[here, 128:256] = part[i, 1]
    grad[...] = jnp.dot(cot_cols[...], active[...], preferred_element_type=f32)
    positive = jnp.where(active[...].astype(f32) > 0, 1.0, 0.0).astype(bf16)
    mid = lax.broadcasted_iota(jnp.int32, (block, 256), 1)
    row = lax.broadcasted_iota(jnp.int32, (block, 256), 0)
    pick = jnp.where(mid == row + first, 1.0, 0.0).astype(bf16)
    mask = lax.dot_general(pick, positive, (((1,), (1,)), ((), ())), preferred_element_type=f32)
    slope[...] = jnp.where(mask > 0.5, 1.0, leak_slope)


def inputs_kernel(place, own, other, own_rims, other_rims, inputs):
    core = place[0]
    for i in range(8):
        for part, rims, at, side in ((own, own_rims, voxels, core), (other, other_rims, 0, 1 - core)):
            here = pl.ds(pl.multiple_of((2 * i + side) * lanes, lanes), lanes)
            middle = part[i, 2]
            scale = jnp.exp2(rims[i, 0:1, at + cols : at + cols + 1] - top)
            at += 128
            rim = [rims[i, :, at + g * 128 : at + (g + 1) * 128] for g in range(8)]
            rim = (jnp.concatenate(rim, axis=0) * scale).astype(bf16)
            inputs[here, 0:128] = jnp.concatenate([rim[:cols], middle[:cols]], axis=0)
            inputs[here, 128:256] = middle
            inputs[here, 256:384] = jnp.concatenate([middle[cols:], rim[cols:]], axis=0)


def split(value):
    high = value.astype(bf16)
    return high, (value - high.astype(f32)).astype(bf16)


def first_kernel(parts, slope, inputs, second, out, scaled, shifted):
    total = jnp.zeros((block, voxels), f32)
    for i in range(8):
        total = total + parts[i, :, :voxels] * jnp.exp2(parts[i, :, voxels : voxels + 1] - top)
    total = total * slope[...]
    power = exponent(total)
    scaled[:, :voxels] = total * jnp.exp2(top - power)
    scaled[:, voxels:] = jnp.broadcast_to(power, (block, 128))
    for c in (-1, 0, 1):
        pair = split(shifted_columns(total, c))
        for b in (-1, 0, 1):
            at = (3 * (b + 1) + c + 1) * 2 * block
            for k in range(2):
                shifted[at + k * block : at + (k + 1) * block, :] = shifted_rows(pair[k], b)
    grad = jnp.dot(shifted[...], inputs[...], preferred_element_type=f32)
    grad = grad.reshape(9, 2, block, 384)
    grad = grad[:, 0] + grad[:, 1]
    power = exponent(grad.reshape(9 * block, 384))
    grad = grad * jnp.exp2(top - power).reshape(1, 1, 1)
    second_power = exponent(second[...])
    other = second[...] * jnp.exp2(top - second_power)
    pieces = [grad[bc, :, a * 128 : (a + 1) * 128] for a in range(3) for bc in range(9)]
    pieces += [other[:, :128], other[:, 128:], jnp.zeros((share * 16 - 3 * taps * block, 128), f32)]
    flat = jnp.concatenate(pieces, axis=0)
    powers = jnp.concatenate(
        [jnp.broadcast_to(power, (8, cols)), jnp.broadcast_to(second_power, (8, cols))], axis=1
    )
    for i in range(16):
        out[i, :share] = flat[i * share : (i + 1) * share]
        out[i, share:] = powers


def sum_kernel(place, sums, out):
    power = sums[0, share:]
    for i in range(1, 16):
        power = jnp.maximum(power, sums[i, share:])
    left = lax.broadcasted_iota(jnp.int32, (8, 128), 1) < cols
    totals = [jnp.zeros((8, 128), f32)] * (share // 8)
    for i in range(16):
        scale = jnp.exp2(sums[i, share:] - power - 4.0)
        turned = pltpu.roll(scale, cols, axis=1)
        first, second = jnp.where(left, scale, turned), jnp.where(left, turned, scale)
        for k in range(share // 8):
            here = jnp.where(place[2] * share + 8 * k < taps * block, first, second)
            totals[k] += sums[i, 8 * k : 8 * k + 8] * here
    for k in range(share // 8):
        out[8 * k : 8 * k + 8] = totals[k]
    out[share:] = power + 4.0


def second_scale_kernel(grad_scale, grad, power, ready, out):
    scale = jnp.exp2(power[0:1, cols : cols + 1] - top) * grad_scale
    out[:, :, :128] = grad[0] * scale.reshape(1, 1, 1)
    out[:, :, 128:] = grad[1] * scale.reshape(1, 1, 1)


def input_kernel(place, blocks, weight, mine, theirs, field):
    core, filt = place[0], place[1]

    def load(target):
        field[...] = jnp.zeros((256, 3 * lanes), f32)
        for j, other in enumerate(block_order):
            source = filt ^ other
            here = pl.ds(pl.multiple_of((source % 2 * 8 + source // 2) * block, block), block)
            scale = jnp.exp2(blocks[j, 0:1, voxels : voxels + 1] - top)
            for b in range(3):
                row = target + b - 1
                at = pl.multiple_of(jnp.clip(row, 0, rows - 1) * lanes, lanes)
                inside = jnp.logical_and(row >= 0, row < rows)
                piece = jnp.where(inside, blocks[j, :, pl.ds(at, lanes)] * scale, 0.0)
                field[here, b * lanes : (b + 1) * lanes] = piece

    def contract(planes_back):
        total = jnp.zeros((len(planes_back) * 128, 2 * lanes), f32)
        for c in (-1, 0, 1):
            pair = split(shifted_columns(field[...], c))
            for b in (-1, 0, 1):
                at = (1 - b) * lanes
                window = jnp.concatenate([half[:, at : at + lanes] for half in pair], axis=1)
                tap = 3 * (b + 1) + c + 1
                taken = jnp.concatenate([weight[9 * a + tap] for a in planes_back], axis=0)
                total += jnp.dot(taken, window, preferred_element_type=f32)
        return (total[:, :lanes] + total[:, lanes:]).T

    for target, out in ((filt, mine), (filt ^ 2, theirs)):
        load(target)
        total = contract((0, 1, 2))
        back, middle, ahead = total[:, :128], total[:, 128:256], total[:, 256:]
        out[0:cols] = middle[:cols] + back[cols:]
        out[cols:lanes] = middle[cols:] + ahead[:cols]
        out[lanes : 3 * cols] = jnp.where(core == 0, ahead[cols:], back[:cols])
        load(target ^ 1)
        rim = contract((jnp.where(core == 0, 2, 0),))
        out[3 * cols :] = jnp.where(core == 0, rim[cols:], rim[:cols])


def edge_kernel(mine, arrived, middle, rims):
    middle[...] = mine[0:lanes] + arrived[0:lanes]
    rims[0] = mine[lanes : 3 * cols] + arrived[lanes : 3 * cols]
    rims[1] = mine[3 * cols :] + arrived[3 * cols :]


def rim_kernel(place, middle, here, there, out):
    core = place[0]
    low, high = (jnp.where(core == side, here[0], there[...]) for side in range(2))
    out[0:cols] = (middle[0:cols] + low).astype(bf16)
    out[cols:] = (middle[cols:] + high).astype(bf16)


def turn_kernel(grad_scale, part, out):
    power = [
        jnp.broadcast_to(part[i, taps * block : taps * block + 1, 0:1], (block, 1)) for i in range(8)
    ]
    scale = jnp.exp2(jnp.concatenate(power, axis=0) - top) * grad_scale
    for t in range(taps):
        here = slice(t * block, (t + 1) * block)
        out[t] = (part[:, here].reshape(128, 128) * scale).T


def gather_kernel(grad_scale, place, own, part, out):
    core = place[0]
    power = [
        jnp.broadcast_to(part[i, taps * block : taps * block + 1, 0:1], (block, 1)) for i in range(8)
    ]
    scale = jnp.exp2(jnp.concatenate(power, axis=0) - top) * grad_scale
    left = pl.ds(pl.multiple_of(core * 128, 128), 128)
    right = pl.ds(pl.multiple_of((1 - core) * 128, 128), 128)
    for t in range(9):
        tap = pl.program_id(0) * 9 + t
        here = pl.ds(pl.multiple_of(tap * block, block), block)
        out[t, :, left] = own[tap]
        out[t, :, right] = (part[:, here].reshape(128, 128) * scale).T


def shards(cotangent, pre_act, layer_input, weight_one, weight_two):
    grad_scale = 1.0 / math.sqrt(voxels * 16)
    filt = lax.axis_index("filt")
    core = filt % 2
    place = jnp.stack([core, filt, lax.axis_index("slab")]).astype(jnp.int32)

    cot = cotangent.transpose(0, 1, 3, 2)
    x = layer_input.reshape(planes, cols, 128)
    pre = pre_act.reshape(planes, cols, 256)
    keep, swap = pl.pallas_call(
        pack_kernel,
        out_shape=[shape((256, 128), bf16)] * 2,
        in_specs=[scalar_spec()] + [pl.BlockSpec()] * 2,
        out_specs=whole(2),
        compiler_params=params(),
        name="pack",
    )(place, cot, x)
    swapped = lax.ppermute(swap, "filt", core_swap)
    here = lax.ppermute(jnp.stack([keep, swapped]), ("slab", "filt"), slab_step)
    there = lax.ppermute(here, "filt", core_swap)
    message = pl.pallas_call(
        message_kernel,
        out_shape=shape((8, 3, 128, 128), bf16),
        in_specs=[pl.BlockSpec()] * 2 + [pl.BlockSpec(memory_space=pl.ANY)],
        out_specs=whole(1)[0],
        compiler_params=params(),
        name="message",
    )(pre, x, swap)
    own_rows = lax.all_to_all(
        message, "filt", split_axis=0, concat_axis=0, tiled=True, axis_index_groups=same_core
    )
    other = lax.ppermute(cot, "filt", core_swap)
    own_w, sent_w = pl.pallas_call(
        weight_kernel,
        out_shape=[shape((128, taps * block), bf16)] * 2,
        in_specs=[scalar_spec()] + [pl.BlockSpec()] + [pl.BlockSpec(memory_space=pl.ANY)],
        out_specs=whole(2),
        compiler_params=params(),
        cost_estimate=cost(12 * 10**9, 1 << 20),
        name="weights",
    )(place, weight_two.transpose(0, 2, 1), here)
    other_w = lax.ppermute(sent_w, "filt", core_swap)

    partial, cot_cols = pl.pallas_call(
        back_kernel,
        out_shape=[shape((8, block, voxels + 1152), f32), shape((taps * block, voxels), bf16)],
        in_specs=[scalar_spec()] + whole(6),
        out_specs=whole(2),
        scratch_shapes=[pltpu.VMEM((taps * block, voxels), bf16)],
        compiler_params=params(),
        cost_estimate=cost(10**10, 4 << 20),
        name="back",
    )(place, cot, other, here, there, own_w, other_w)
    partial = partial.astype(f16)
    own_rows, _ = lax.optimization_barrier((own_rows, partial))
    parts = lax.all_to_all(
        partial, "filt", split_axis=0, concat_axis=0, tiled=True, axis_index_groups=same_core
    )
    other_rows = lax.ppermute(own_rows, "filt", core_swap)
    second, slope = pl.pallas_call(
        second_kernel,
        out_shape=[shape((taps * block, 256), f32), shape((block, voxels), f32)],
        in_specs=[scalar_spec()] + whole(3),
        out_specs=whole(2),
        scratch_shapes=[pltpu.VMEM((voxels, 256), bf16)],
        compiler_params=params(),
        cost_estimate=cost(2 * 432 * 2048 * 256, 6 << 20),
        name="second",
    )(place, cot_cols, own_rows, other_rows)
    parts, _ = lax.optimization_barrier((parts, second))
    other_rims = lax.ppermute(parts, "filt", core_swap)[:, :, voxels:].astype(f32)
    parts = parts.astype(f32)
    inputs = pl.pallas_call(
        inputs_kernel,
        out_shape=shape((voxels, 384), bf16),
        in_specs=[scalar_spec()] + whole(4),
        out_specs=whole(1)[0],
        compiler_params=params(),
        cost_estimate=cost(10**7, 1 << 20),
        name="inputs",
    )(place, own_rows, other_rows, parts, other_rims)

    merged, scaled = pl.pallas_call(
        first_kernel,
        out_shape=[shape((16, share + 8, 128), f32), shape((block, voxels + 128), f32)],
        in_specs=whole(4),
        out_specs=whole(2),
        scratch_shapes=[pltpu.VMEM((18 * block, voxels), bf16)],
        compiler_params=params(),
        cost_estimate=cost(2 * 288 * 2048 * 384, 6 << 20),
        name="first",
    )(parts, slope, inputs, second)
    merged = merged.astype(f16)
    sums = lax.all_to_all(merged, "slab", split_axis=0, concat_axis=0, tiled=True)

    blocks, _ = lax.optimization_barrier((scaled.astype(f16)[None], inputs))
    for together in swaps:
        arrived = [
            lax.ppermute(blocks, "filt", [(i, i ^ swap) for i in range(16)]) for swap in together
        ]
        blocks = jnp.concatenate([blocks] + arrived, axis=0)
    mine_x0, theirs_x0 = pl.pallas_call(
        input_kernel,
        out_shape=[shape((2 * lanes, 128), f32)] * 2,
        in_specs=[scalar_spec()] + whole(2),
        out_specs=whole(2),
        scratch_shapes=[pltpu.VMEM((256, 3 * lanes), f32)],
        compiler_params=params(),
        cost_estimate=cost(4 * 128 * 256 * 256 * taps, 4 << 20),
        name="input",
    )(place, blocks.astype(f32), weight_one)
    arrived_x0 = lax.ppermute(theirs_x0, "filt", z_swap)
    mine = pl.pallas_call(
        sum_kernel,
        out_shape=shape((share + 8, 128), f32),
        in_specs=[scalar_spec()] + whole(1),
        out_specs=whole(1)[0],
        compiler_params=params(),
        name="sum",
    )(place, sums.astype(f32))
    near = jnp.broadcast_to(mine.astype(f16)[None], (16, share + 8, 128))
    near = lax.all_to_all(near, "slab", split_axis=0, concat_axis=0, tiled=True)
    near, arrived_x0 = lax.optimization_barrier((near, arrived_x0))
    middle, rims = pl.pallas_call(
        edge_kernel,
        out_shape=[shape((lanes, 128), f32), shape((2, cols, 128), f32)],
        in_specs=whole(2),
        out_specs=whole(2),
        compiler_params=params(),
        name="edge",
    )(mine_x0, arrived_x0)
    rims = lax.ppermute(rims, ("slab", "filt"), slab_step)
    other_rim = lax.ppermute(rims[1], "filt", core_swap)
    grad_x0 = pl.pallas_call(
        rim_kernel,
        out_shape=shape((lanes, 128), bf16),
        in_specs=[scalar_spec()] + whole(3),
        out_specs=whole(1)[0],
        compiler_params=params(),
        name="rim",
    )(place, middle, rims, other_rim).reshape(planes, 1, cols, 128)
    flat = near[:, :share].reshape(16 * share, 128)
    power = near[0, share:]
    wide = jnp.concatenate([flat[: taps * block], power], axis=0)
    wide = jnp.broadcast_to(wide[None], (8, taps * block + 8, 128))
    wide = lax.all_to_all(
        wide, "filt", split_axis=0, concat_axis=0, tiled=True, axis_index_groups=same_core
    )
    wide, grad_x0 = lax.optimization_barrier((wide, grad_x0))
    other_wide = lax.ppermute(wide, "filt", core_swap)
    own_wide = wide.astype(f32)
    grad_w2 = pl.pallas_call(
        functools.partial(second_scale_kernel, grad_scale),
        out_shape=shape((taps, block, 256), f32),
        in_specs=whole(2) + [pl.BlockSpec(memory_space=pl.ANY)],
        out_specs=whole(1)[0],
        compiler_params=params(),
        cost_estimate=cost(5 * 10**9, 1 << 20),
        name="second_scale",
    )(
        flat[taps * block : 3 * taps * block].reshape(2, taps, block, 128).astype(f32),
        power.astype(f32),
        own_wide,
    ).transpose(0, 2, 1)
    turned = pl.pallas_call(
        functools.partial(turn_kernel, grad_scale),
        out_shape=shape((taps, 128, 128), f32),
        in_specs=whole(1),
        out_specs=whole(1)[0],
        compiler_params=params(),
        cost_estimate=cost(10**9, 1 << 20),
        name="turn",
    )(own_wide)
    grad_w1 = pl.pallas_call(
        functools.partial(gather_kernel, grad_scale),
        out_shape=shape((taps, 128, 256), f32),
        grid=(3,),
        in_specs=[scalar_spec()] + whole(2),
        out_specs=pl.BlockSpec((9, 128, 256), lambda i: (i, 0, 0)),
        compiler_params=params(),
        name="gather",
    )(place, turned, other_wide.astype(f32))
    return (grad_w2, grad_w1, grad_x0)


def solution(mesh):
    return jax.shard_map(
        shards,
        mesh=mesh,
        in_specs=(
            P("slab", None, None, "filt"),
            P("slab", "filt", None, None),
            P("slab", "filt", None, None),
            P(),
            P(None, None, "filt"),
        ),
        out_specs=(P(None, None, "filt"), P(), P("slab", "filt", None, None)),
        check_vma=False,
    )
```

```python
import functools
import math

import jax
import jax.numpy as jnp
from jax import lax
from jax.experimental import pallas as pl
from jax.experimental.pallas import tpu as pltpu
from jax.sharding import PartitionSpec as P

leak_slope = 0.3
bf16 = jnp.bfloat16
f32 = jnp.float32
f16 = jnp.float16
top = 13.0
planes, rows, cols = 2, 16, 64
lanes = planes * cols
voxels = rows * lanes
block = 16
taps = 27

same_core = [[2 * i + core for i in range(8)] for core in range(2)]
z_swap = [(i, i ^ 2) for i in range(16)]
core_swap = [(i, i ^ 1) for i in range(16)]
share = 88
swaps = ((4,), (12,), (1,))
block_order = [0]
for together in swaps:
    block_order += [other ^ swap for swap in together for other in block_order]
slab_step = [(s * 16 + f, (s + 1) * 16 + f) for s in range(15) for f in range(0, 16, 2)]
slab_step += [((s + 1) * 16 + f, s * 16 + f) for s in range(15) for f in range(1, 16, 2)]


def params(limit=48):
    return pltpu.CompilerParams(vmem_limit_bytes=limit * 1024 * 1024)


def cost(flops, moved):
    return pl.CostEstimate(flops=flops, bytes_accessed=moved, transcendentals=0)


def shape(dims, dtype):
    return jax.ShapeDtypeStruct(dims, dtype)


def whole(count):
    return [pl.BlockSpec(memory_space=pltpu.VMEM)] * count


def scalar_spec():
    return pl.BlockSpec(memory_space=pltpu.SMEM)


def exponent(value):
    most = jnp.max(jnp.max(jnp.abs(value), axis=0, keepdims=True), axis=1, keepdims=True)
    return jnp.ceil(jnp.log2(jnp.maximum(most, 2.0**-100)))


def weight_kernel(place, weight, ready, own, sent):
    flat = weight[...].astype(f32).reshape(taps * block, 256).T.astype(bf16)
    low, high = flat[:128], flat[128:]
    own[...] = jnp.where(place[0] == 0, low, high)
    sent[...] = jnp.where(place[0] == 0, high, low)


def pack_kernel(place, cot, x, keep, swap):
    core = place[0]
    for plane, out in ((1 - core, keep), (core, swap)):
        field = cot[plane].reshape(rows * block, cols)
        piece = x[plane]
        side = jnp.concatenate(
            [piece[:, :cols], piece[:, cols:], jnp.zeros((2 * cols, cols), bf16)], axis=0
        )
        out[...] = jnp.concatenate([field, side], axis=1)


def stack_kernel(keep, swapped, ready, out):
    out[0] = keep[...]
    out[1] = swapped[...]


def message_kernel(far_pre, far_x, packed, out, pre, x, sems):
    copies = [
        pltpu.make_async_copy(far_pre, pre, sems.at[0]),
        pltpu.make_async_copy(far_x, x, sems.at[1]),
    ]
    for copy in copies:
        copy.start()
    for copy in copies:
        copy.wait()
    value = pre[...].astype(f32).reshape(lanes, 256)
    active = jnp.where(value > 0, value, leak_slope * value).astype(bf16)
    own = x[...].reshape(lanes, 128)
    for i in range(8):
        out[i, 0] = active[:, :128]
        out[i, 1] = active[:, 128:]
        out[i, 2] = own


def shifted_rows(field, b):
    gap = jnp.zeros((field.shape[0], lanes), field.dtype)
    if b == 1:
        return jnp.concatenate([gap, field[:, :-lanes]], axis=1)
    if b == -1:
        return jnp.concatenate([field[:, lanes:], gap], axis=1)
    return field


def shifted_columns(field, c):
    if c == 0:
        return field
    width = field.shape[1]
    col = lax.broadcasted_iota(jnp.int32, field.shape, 1) % cols
    edge = 0 if c == 1 else cols - 1
    return jnp.where(col == edge, jnp.zeros_like(field), pltpu.roll(field, c % width, axis=1))


def fill_columns(own, low, high, out):
    below = low[:, :cols].reshape(rows, block, cols)
    above = high[:, :cols].reshape(rows, block, cols)
    parts = [below, own[0], own[1], above]
    for a in (-1, 0, 1):
        pieces = []
        for r in range(rows):
            pieces += [parts[1 - a][r].astype(f32), parts[2 - a][r].astype(f32)]
        field = jnp.concatenate(
            [jnp.concatenate(pieces[2 * r : 2 * r + 2], axis=1) for r in range(rows)], axis=1
        )
        for c in (-1, 0, 1):
            moved = shifted_columns(field, c).astype(bf16)
            for b in (-1, 0, 1):
                tap = 9 * (a + 1) + 3 * (b + 1) + c + 1
                out[tap * block : (tap + 1) * block, :] = shifted_rows(moved, b)


def back_kernel(place, own, other, here, there, own_w, other_w, out, cot_cols, other_cols):
    core = place[0]
    own_low, own_high = (jnp.where(core == side, here[0], there[1]) for side in range(2))
    other_low, other_high = (jnp.where(core == side, here[1], there[0]) for side in range(2))
    fill_columns(own, own_low, own_high, cot_cols)
    fill_columns(other, other_low, other_high, other_cols)
    total = jnp.dot(own_w[...], cot_cols[...], preferred_element_type=f32)
    total += jnp.dot(other_w[...], other_cols[...], preferred_element_type=f32)
    power = exponent(total)
    out[:, :, :voxels] = (total * jnp.exp2(top - power)).reshape(8, block, voxels)
    rims = [
        jnp.concatenate([pack[0:cols, cols:], pack[cols : 2 * cols, cols:]], axis=1)
        for pack in (own_low, own_high)
    ]
    rim = jnp.concatenate(rims, axis=0).astype(f32)
    rim_power = exponent(rim)
    rim = rim * jnp.exp2(top - rim_power)
    side = [
        jnp.broadcast_to(power, (block, cols)),
        jnp.broadcast_to(rim_power, (block, cols)),
    ] + [rim[g * block : (g + 1) * block] for g in range(8)]
    side = jnp.concatenate(side, axis=1)
    for i in range(8):
        out[i, :, voxels:] = side


def second_kernel(place, cot_cols, own, other, grad, slope, active):
    core = place[0]
    first = place[0] * 128 + place[1] // 2 * block
    for i in range(8):
        for part, side in ((own, core), (other, 1 - core)):
            here = pl.ds(pl.multiple_of((2 * i + side) * lanes, lanes), lanes)
            active[here, 0:128] = part[i, 0]
            active[here, 128:256] = part[i, 1]
    grad[...] = jnp.dot(cot_cols[...], active[...], preferred_element_type=f32)
    positive = jnp.where(active[...].astype(f32) > 0, 1.0, 0.0).astype(bf16)
    mid = lax.broadcasted_iota(jnp.int32, (block, 256), 1)
    row = lax.broadcasted_iota(jnp.int32, (block, 256), 0)
    pick = jnp.where(mid == row + first, 1.0, 0.0).astype(bf16)
    mask = lax.dot_general(pick, positive, (((1,), (1,)), ((), ())), preferred_element_type=f32)
    slope[...] = jnp.where(mask > 0.5, 1.0, leak_slope)


def inputs_kernel(place, own, other, own_rims, other_rims, inputs):
    core = place[0]
    for i in range(8):
        for part, rims, at, side in ((own, own_rims, voxels, core), (other, other_rims, 0, 1 - core)):
            here = pl.ds(pl.multiple_of((2 * i + side) * lanes, lanes), lanes)
            middle = part[i, 2]
            scale = jnp.exp2(rims[i, 0:1, at + cols : at + cols + 1] - top)
            at += 128
            rim = [rims[i, :, at + g * 128 : at + (g + 1) * 128] for g in range(8)]
            rim = (jnp.concatenate(rim, axis=0) * scale).astype(bf16)
            inputs[here, 0:128] = jnp.concatenate([rim[:cols], middle[:cols]], axis=0)
            inputs[here, 128:256] = middle
            inputs[here, 256:384] = jnp.concatenate([middle[cols:], rim[cols:]], axis=0)


def split(value):
    high = value.astype(bf16)
    return high, (value - high.astype(f32)).astype(bf16)


def first_kernel(parts, slope, inputs, second, out, scaled, shifted):
    total = jnp.zeros((block, voxels), f32)
    for i in range(8):
        total = total + parts[i, :, :voxels] * jnp.exp2(parts[i, :, voxels : voxels + 1] - top)
    total = total * slope[...]
    power = exponent(total)
    scaled[:, :voxels] = total * jnp.exp2(top - power)
    scaled[:, voxels:] = jnp.broadcast_to(power, (block, 128))
    for c in (-1, 0, 1):
        pair = split(shifted_columns(total, c))
        for b in (-1, 0, 1):
            at = (3 * (b + 1) + c + 1) * 2 * block
            for k in range(2):
                shifted[at + k * block : at + (k + 1) * block, :] = shifted_rows(pair[k], b)
    grad = jnp.dot(shifted[...], inputs[...], preferred_element_type=f32)
    grad = grad.reshape(9, 2, block, 384)
    grad = grad[:, 0] + grad[:, 1]
    power = exponent(grad.reshape(9 * block, 384))
    grad = grad * jnp.exp2(top - power).reshape(1, 1, 1)
    second_power = exponent(second[...])
    other = second[...] * jnp.exp2(top - second_power)
    pieces = [grad[bc, :, a * 128 : (a + 1) * 128] for a in range(3) for bc in range(9)]
    pieces += [other[:, :128], other[:, 128:], jnp.zeros((share * 16 - 3 * taps * block, 128), f32)]
    flat = jnp.concatenate(pieces, axis=0)
    powers = jnp.concatenate(
        [jnp.broadcast_to(power, (8, cols)), jnp.broadcast_to(second_power, (8, cols))], axis=1
    )
    for i in range(16):
        out[i, :share] = flat[i * share : (i + 1) * share]
        out[i, share:] = powers


def sum_kernel(place, sums, out):
    power = sums[0, share:]
    for i in range(1, 16):
        power = jnp.maximum(power, sums[i, share:])
    left = lax.broadcasted_iota(jnp.int32, (8, 128), 1) < cols
    totals = [jnp.zeros((8, 128), f32)] * (share // 8)
    for i in range(16):
        scale = jnp.exp2(sums[i, share:] - power - 4.0)
        turned = pltpu.roll(scale, cols, axis=1)
        first, second = jnp.where(left, scale, turned), jnp.where(left, turned, scale)
        for k in range(share // 8):
            here = jnp.where(place[2] * share + 8 * k < taps * block, first, second)
            totals[k] += sums[i, 8 * k : 8 * k + 8] * here
    for k in range(share // 8):
        out[8 * k : 8 * k + 8] = totals[k]
    out[share:] = power + 4.0


def second_scale_kernel(grad_scale, grad, power, ready, out):
    scale = jnp.exp2(power[0:1, cols : cols + 1] - top) * grad_scale
    out[:, :, :128] = grad[0] * scale.reshape(1, 1, 1)
    out[:, :, 128:] = grad[1] * scale.reshape(1, 1, 1)


def input_kernel(place, blocks, weight, mine, theirs, field):
    core, filt = place[0], place[1]

    def load(target):
        field[...] = jnp.zeros((256, 3 * lanes), f32)
        for j, other in enumerate(block_order):
            source = filt ^ other
            here = pl.ds(pl.multiple_of((source % 2 * 8 + source // 2) * block, block), block)
            scale = jnp.exp2(blocks[j, 0:1, voxels : voxels + 1] - top)
            for b in range(3):
                row = target + b - 1
                at = pl.multiple_of(jnp.clip(row, 0, rows - 1) * lanes, lanes)
                inside = jnp.logical_and(row >= 0, row < rows)
                piece = jnp.where(inside, blocks[j, :, pl.ds(at, lanes)] * scale, 0.0)
                field[here, b * lanes : (b + 1) * lanes] = piece

    def contract(planes_back):
        total = jnp.zeros((len(planes_back) * 128, 2 * lanes), f32)
        for c in (-1, 0, 1):
            pair = split(shifted_columns(field[...], c))
            for b in (-1, 0, 1):
                at = (1 - b) * lanes
                window = jnp.concatenate([half[:, at : at + lanes] for half in pair], axis=1)
                tap = 3 * (b + 1) + c + 1
                taken = jnp.concatenate([weight[9 * a + tap] for a in planes_back], axis=0)
                total += jnp.dot(taken, window, preferred_element_type=f32)
        return (total[:, :lanes] + total[:, lanes:]).T

    for target, out in ((filt, mine), (filt ^ 2, theirs)):
        load(target)
        total = contract((0, 1, 2))
        back, middle, ahead = total[:, :128], total[:, 128:256], total[:, 256:]
        out[0:cols] = middle[:cols] + back[cols:]
        out[cols:lanes] = middle[cols:] + ahead[:cols]
        out[lanes : 3 * cols] = jnp.where(core == 0, ahead[cols:], back[:cols])
        load(target ^ 1)
        rim = contract((jnp.where(core == 0, 2, 0),))
        out[3 * cols :] = jnp.where(core == 0, rim[cols:], rim[:cols])


def edge_kernel(mine, arrived, middle, rims):
    middle[...] = mine[0:lanes] + arrived[0:lanes]
    rims[0] = mine[lanes : 3 * cols] + arrived[lanes : 3 * cols]
    rims[1] = mine[3 * cols :] + arrived[3 * cols :]


def rim_kernel(place, middle, here, there, out):
    core = place[0]
    low, high = (jnp.where(core == side, here[0], there[...]) for side in range(2))
    out[0:cols] = (middle[0:cols] + low).astype(bf16)
    out[cols:] = (middle[cols:] + high).astype(bf16)


def turn_kernel(grad_scale, part, out):
    power = [
        jnp.broadcast_to(part[i, taps * block : taps * block + 1, 0:1], (block, 1)) for i in range(8)
    ]
    scale = jnp.exp2(jnp.concatenate(power, axis=0) - top) * grad_scale
    for t in range(taps):
        here = slice(t * block, (t + 1) * block)
        out[t] = (part[:, here].reshape(128, 128) * scale).T


def gather_kernel(grad_scale, place, own, part, out):
    core = place[0]
    power = [
        jnp.broadcast_to(part[i, taps * block : taps * block + 1, 0:1], (block, 1)) for i in range(8)
    ]
    scale = jnp.exp2(jnp.concatenate(power, axis=0) - top) * grad_scale
    left = pl.ds(pl.multiple_of(core * 128, 128), 128)
    right = pl.ds(pl.multiple_of((1 - core) * 128, 128), 128)
    for t in range(9):
        tap = pl.program_id(0) * 9 + t
        here = pl.ds(pl.multiple_of(tap * block, block), block)
        out[t, :, left] = own[tap]
        out[t, :, right] = (part[:, here].reshape(128, 128) * scale).T


def shards(cotangent, pre_act, layer_input, weight_one, weight_two):
    grad_scale = 1.0 / math.sqrt(voxels * 16)
    filt = lax.axis_index("filt")
    core = filt % 2
    place = jnp.stack([core, filt, lax.axis_index("slab")]).astype(jnp.int32)

    cot = cotangent.transpose(0, 1, 3, 2)
    x = layer_input.reshape(planes, cols, 128)
    pre = pre_act.reshape(planes, cols, 256)
    keep, swap = pl.pallas_call(
        pack_kernel,
        out_shape=[shape((256, 128), bf16)] * 2,
        in_specs=[scalar_spec()] + [pl.BlockSpec()] * 2,
        out_specs=whole(2),
        compiler_params=params(),
        name="pack",
    )(place, cot, x)
    swapped = lax.ppermute(swap, "filt", core_swap)
    message = pl.pallas_call(
        message_kernel,
        out_shape=shape((8, 3, 128, 128), bf16),
        in_specs=[pl.BlockSpec(memory_space=pl.ANY)] * 3,
        out_specs=whole(1)[0],
        scratch_shapes=[
            pltpu.VMEM((planes, cols, 256), bf16),
            pltpu.VMEM((planes, cols, 128), bf16),
            pltpu.SemaphoreType.DMA((2,)),
        ],
        compiler_params=params(60),
        name="message",
    )(pre, x, swap)
    both = pl.pallas_call(
        stack_kernel,
        out_shape=shape((2, 256, 128), bf16),
        in_specs=whole(2) + [pl.BlockSpec(memory_space=pl.ANY)],
        out_specs=whole(1)[0],
        compiler_params=params(),
        name="stack",
    )(keep, swapped, message)
    here = lax.ppermute(both, ("slab", "filt"), slab_step)
    there = lax.ppermute(here, "filt", core_swap)
    own_rows = lax.all_to_all(
        message, "filt", split_axis=0, concat_axis=0, tiled=True, axis_index_groups=same_core
    )
    other = lax.ppermute(cot, "filt", core_swap)
    own_w, sent_w = pl.pallas_call(
        weight_kernel,
        out_shape=[shape((128, taps * block), bf16)] * 2,
        in_specs=[scalar_spec()] + [pl.BlockSpec()] + [pl.BlockSpec(memory_space=pl.ANY)],
        out_specs=whole(2),
        compiler_params=params(),
        cost_estimate=cost(12 * 10**9, 1 << 20),
        name="weights",
    )(place, weight_two.transpose(0, 2, 1), here)
    other_w = lax.ppermute(sent_w, "filt", core_swap)

    partial, cot_cols = pl.pallas_call(
        back_kernel,
        out_shape=[shape((8, block, voxels + 1152), f32), shape((taps * block, voxels), bf16)],
        in_specs=[scalar_spec()] + whole(6),
        out_specs=whole(2),
        scratch_shapes=[pltpu.VMEM((taps * block, voxels), bf16)],
        compiler_params=params(),
        cost_estimate=cost(10**10, 4 << 20),
        name="back",
    )(place, cot, other, here, there, own_w, other_w)
    partial = partial.astype(f16)
    own_rows, _ = lax.optimization_barrier((own_rows, partial))
    parts = lax.all_to_all(
        partial, "filt", split_axis=0, concat_axis=0, tiled=True, axis_index_groups=same_core
    )
    other_rows = lax.ppermute(own_rows, "filt", core_swap)
    second, slope = pl.pallas_call(
        second_kernel,
        out_shape=[shape((taps * block, 256), f32), shape((block, voxels), f32)],
        in_specs=[scalar_spec()] + whole(3),
        out_specs=whole(2),
        scratch_shapes=[pltpu.VMEM((voxels, 256), bf16)],
        compiler_params=params(),
        cost_estimate=cost(2 * 432 * 2048 * 256, 6 << 20),
        name="second",
    )(place, cot_cols, own_rows, other_rows)
    parts, _ = lax.optimization_barrier((parts, second))
    other_rims = lax.ppermute(parts, "filt", core_swap)[:, :, voxels:].astype(f32)
    parts = parts.astype(f32)
    inputs = pl.pallas_call(
        inputs_kernel,
        out_shape=shape((voxels, 384), bf16),
        in_specs=[scalar_spec()] + whole(4),
        out_specs=whole(1)[0],
        compiler_params=params(),
        cost_estimate=cost(10**7, 1 << 20),
        name="inputs",
    )(place, own_rows, other_rows, parts, other_rims)

    merged, scaled = pl.pallas_call(
        first_kernel,
        out_shape=[shape((16, share + 8, 128), f32), shape((block, voxels + 128), f32)],
        in_specs=whole(4),
        out_specs=whole(2),
        scratch_shapes=[pltpu.VMEM((18 * block, voxels), bf16)],
        compiler_params=params(),
        cost_estimate=cost(2 * 288 * 2048 * 384, 6 << 20),
        name="first",
    )(parts, slope, inputs, second)
    merged = merged.astype(f16)
    sums = lax.all_to_all(merged, "slab", split_axis=0, concat_axis=0, tiled=True)

    blocks, _ = lax.optimization_barrier((scaled.astype(f16)[None], inputs))
    for together in swaps:
        arrived = [
            lax.ppermute(blocks, "filt", [(i, i ^ swap) for i in range(16)]) for swap in together
        ]
        blocks = jnp.concatenate([blocks] + arrived, axis=0)
    mine_x0, theirs_x0 = pl.pallas_call(
        input_kernel,
        out_shape=[shape((2 * lanes, 128), f32)] * 2,
        in_specs=[scalar_spec()] + whole(2),
        out_specs=whole(2),
        scratch_shapes=[pltpu.VMEM((256, 3 * lanes), f32)],
        compiler_params=params(),
        cost_estimate=cost(4 * 128 * 256 * 256 * taps, 4 << 20),
        name="input",
    )(place, blocks.astype(f32), weight_one)
    arrived_x0 = lax.ppermute(theirs_x0, "filt", z_swap)
    mine = pl.pallas_call(
        sum_kernel,
        out_shape=shape((share + 8, 128), f32),
        in_specs=[scalar_spec()] + whole(1),
        out_specs=whole(1)[0],
        compiler_params=params(),
        name="sum",
    )(place, sums.astype(f32))
    near = jnp.broadcast_to(mine.astype(f16)[None], (16, share + 8, 128))
    near = lax.all_to_all(near, "slab", split_axis=0, concat_axis=0, tiled=True)
    near, arrived_x0 = lax.optimization_barrier((near, arrived_x0))
    middle, rims = pl.pallas_call(
        edge_kernel,
        out_shape=[shape((lanes, 128), f32), shape((2, cols, 128), f32)],
        in_specs=whole(2),
        out_specs=whole(2),
        compiler_params=params(),
        name="edge",
    )(mine_x0, arrived_x0)
    rims = lax.ppermute(rims, ("slab", "filt"), slab_step)
    other_rim = lax.ppermute(rims[1], "filt", core_swap)
    grad_x0 = pl.pallas_call(
        rim_kernel,
        out_shape=shape((lanes, 128), bf16),
        in_specs=[scalar_spec()] + whole(3),
        out_specs=whole(1)[0],
        compiler_params=params(),
        name="rim",
    )(place, middle, rims, other_rim).reshape(planes, 1, cols, 128)
    flat = near[:, :share].reshape(16 * share, 128)
    power = near[0, share:]
    wide = jnp.concatenate([flat[: taps * block], power], axis=0)
    wide = jnp.broadcast_to(wide[None], (8, taps * block + 8, 128))
    wide = lax.all_to_all(
        wide, "filt", split_axis=0, concat_axis=0, tiled=True, axis_index_groups=same_core
    )
    wide, grad_x0 = lax.optimization_barrier((wide, grad_x0))
    other_wide = lax.ppermute(wide, "filt", core_swap)
    own_wide = wide.astype(f32)
    grad_w2 = pl.pallas_call(
        functools.partial(second_scale_kernel, grad_scale),
        out_shape=shape((taps, block, 256), f32),
        in_specs=whole(2) + [pl.BlockSpec(memory_space=pl.ANY)],
        out_specs=whole(1)[0],
        compiler_params=params(),
        cost_estimate=cost(5 * 10**9, 1 << 20),
        name="second_scale",
    )(
        flat[taps * block : 3 * taps * block].reshape(2, taps, block, 128).astype(f32),
        power.astype(f32),
        own_wide,
    ).transpose(0, 2, 1)
    turned = pl.pallas_call(
        functools.partial(turn_kernel, grad_scale),
        out_shape=shape((taps, 128, 128), f32),
        in_specs=whole(1),
        out_specs=whole(1)[0],
        compiler_params=params(),
        cost_estimate=cost(10**9, 1 << 20),
        name="turn",
    )(own_wide)
    grad_w1 = pl.pallas_call(
        functools.partial(gather_kernel, grad_scale),
        out_shape=shape((taps, 128, 256), f32),
        grid=(3,),
        in_specs=[scalar_spec()] + whole(2),
        out_specs=pl.BlockSpec((9, 128, 256), lambda i: (i, 0, 0)),
        compiler_params=params(),
        name="gather",
    )(place, turned, other_wide.astype(f32))
    return (grad_w2, grad_w1, grad_x0)


def solution(mesh):
    return jax.shard_map(
        shards,
        mesh=mesh,
        in_specs=(
            P("slab", None, None, "filt"),
            P("slab", "filt", None, None),
            P("slab", "filt", None, None),
            P(),
            P(None, None, "filt"),
        ),
        out_specs=(P(None, None, "filt"), P(), P("slab", "filt", None, None)),
        check_vma=False,
    )
```
